32 devices in a mesh: box: 32 (over z, y, x, core).
Axes of the slice: x: 2, y: 2, z: 4, core: 2. Of those that a mesh axis runs over, the one named last changes fastest.
Arguments:
- sources: float32 [2048, 32768], P(None, 'box'), may hold values from -6 to 6
- leaf_basis: bfloat16 [64, 512, 256], P('box'), may hold values from -0.25 to 0.25
- stay_blocks: bfloat16 [6, 64, 256, 256], P(None, 'box'), may hold values from -0.25 to 0.25
- cross_blocks: bfloat16 [6, 64, 256, 256], P(None, 'box'), may hold values from -0.25 to 0.25
- out_basis: bfloat16 [64, 256, 512], P('box'), may hold values from -0.375 to 0.375
- near_blocks: bfloat16 [64, 768, 512], P('box'), may hold values from -0.21875 to 0.21875
Outputs:
- targets: float32 [2048, 32768], P(None, 'box')
The draws below stay inside these ranges and needn't reach their ends.
All inputs are finite; a program needn't handle non-finite values.
Results may differ from the reference program's by a relative error of at most 0.014.
Values may be sent and summed in bfloat16 or wider, within the bound.
No kernel may reach another device: no remote copies, remote signals or barrier semaphores. Data moves between devices by JAX's collectives and lax.ppermute only.
A program may use at most 128 MiB of HBM per device.

```python
import jax
import jax.numpy as jnp

R = 256
B = 512
NV = 2048
H = 128
BOXES = 64
LEVELS = 6
POINTS = 32768


def steps_of(key, shape, split, least, top_value):
    loudness = 1.0
    for axis_at, blocks in split:
        heights = jax.random.uniform(jax.random.fold_in(jax.random.fold_in(key, 6), axis_at), (blocks,), jnp.float32, least / len(split), top_value / len(split))
        loudness = loudness * jnp.repeat(jnp.exp(heights), shape[axis_at] // blocks).reshape((-1,) + (1,) * (len(shape) - 1 - axis_at))
    return loudness


def normal_values(stream_key, extent, scale, most, split=(), kind=jnp.bfloat16):
    factor_of = steps_of(stream_key, extent, split, -0.22, 0.18) if split else 1.0
    drawn = jax.random.normal(stream_key, extent, jnp.float32) * scale * factor_of
    return jnp.minimum(jnp.maximum(drawn, -most), most).astype(kind)


def setup_inputs(seed: int = 0) -> dict:
    streams_of = jax.random.split(jax.random.key(seed), 7)
    sources = normal_values(streams_of[0], (NV, POINTS), 1.0, 6.0, ((1, 32),), jnp.float32)
    leaf_basis = normal_values(streams_of[1], (BOXES, B, R), B ** -0.5, 0.25, ((0, 32),))
    stay_blocks = normal_values(streams_of[2], (LEVELS, BOXES, R, R), (2 * R) ** -0.5, 0.25, ((1, 32),))
    cross_blocks = normal_values(streams_of[3], (LEVELS, BOXES, R, R), (2 * R) ** -0.5, 0.25, ((1, 32),))
    out_basis = normal_values(streams_of[4], (BOXES, R, B), R ** -0.5, 0.375, ((0, 32),))
    near_blocks = normal_values(streams_of[5], (BOXES, B + 2 * H, B), (B + 2 * H) ** -0.5, 0.21875, ((0, 32),))
    return dict(sources=sources, leaf_basis=leaf_basis, stay_blocks=stay_blocks, cross_blocks=cross_blocks, out_basis=out_basis, near_blocks=near_blocks)


def reference(sources, leaf_basis, stay_blocks, cross_blocks, out_basis, near_blocks):
    rounded = sources.astype(jnp.bfloat16)
    blocked = rounded.astype(jnp.float32).reshape(NV, BOXES, B)
    proxies = jnp.einsum("nbc,bcr->bnr", blocked, leaf_basis.astype(jnp.float32)).astype(jnp.bfloat16)
    for depth_at in range(LEVELS):
        wide = proxies.astype(jnp.float32)
        stay = jnp.einsum("bnr,brs->bns", wide, stay_blocks[depth_at].astype(jnp.float32))
        moved = jnp.einsum("bnr,brs->bns", wide, cross_blocks[depth_at].astype(jnp.float32))
        stride = 2 ** depth_at
        moved = moved.reshape(BOXES // (2 * stride), 2, stride, NV, R)[:, ::-1].reshape(BOXES, NV, R)
        proxies = (stay + moved).astype(jnp.bfloat16)
    far_field = jnp.einsum("bnr,brc->nbc", proxies.astype(jnp.float32), out_basis.astype(jnp.float32))
    padded = jnp.pad(rounded, ((0, 0), (H, H)))
    middle = padded[:, H:H + POINTS].reshape(NV, BOXES, B)
    left_rim = padded[:, :POINTS].reshape(NV, BOXES, B)[:, :, :H]
    right_rim = padded[:, 2 * H:2 * H + POINTS].reshape(NV, BOXES, B)[:, :, B - H:]
    window = jnp.concatenate([left_rim, middle, right_rim], axis=2).astype(jnp.float32)
    near_field = jnp.einsum("nbw,bwc->nbc", window, near_blocks.astype(jnp.float32))
    return (far_field + near_field).reshape(NV, POINTS)
```

```python
import functools

import jax
import jax.numpy as jnp
from jax import lax
from jax.experimental import pallas as pl
from jax.experimental.pallas import tpu as pltpu
from jax.sharding import PartitionSpec as P

BF16 = jnp.bfloat16
F32 = jnp.float32
FIRST = (23,22,22,21,20,20)
MIDDLE = FIRST
LAST = FIRST


def dot(a, b):
    return jnp.dot(a, b, preferred_element_type=F32)


def cut(rows, shares):
    ends = [rows * sum(shares[: at + 1]) // sum(shares) // 16 * 16 for at in range(len(shares))]
    ends[-1] = rows
    starts = [0] + ends[:-1]
    return [(start, end - start) for start, end in zip(starts, ends)]


def inside(piece, pieces):
    return [q for q in pieces if piece[0] <= q[0] and q[0] + q[1] <= piece[0] + piece[1]]


RIMS = (-1, (0, 0))
IN_FLIGHT = 5


RIMS = (-1, (0, 0))
TAKE = (-2, (0, 0))


def order_of(cuts, rows):
    levels = len(cuts)
    pieces = cuts[1]
    order = []
    for t in range(len(pieces) + levels - 1):
        for level in [levels - 2, levels - 1] + list(range(levels - 3, -1, -1)):
            if 0 <= t - level < len(pieces):
                order.append((level, pieces[t - level]))
        if t == 1:
            order.append(RIMS)
        if t == 2:
            order.append(TAKE)
    return order, 0


def copies(pairs, sems):
    return [pltpu.make_async_copy(src, dst, sems.at[at]) for at, (src, dst) in enumerate(pairs)]


def blocks_of(size):
    step = 128
    return [(at, min(step, size - at)) for at in range(0, size, step)]


def leaf_rows(src, leaf, stay, cross, held, sent, rows):
    points, rank = leaf.shape[1:]
    grown = [
        dot(src[rows, b * points : (b + 1) * points].astype(BF16), leaf[b]).astype(BF16) for b in range(2)
    ]
    for b in range(2):
        cols = slice(b * rank, (b + 1) * rank)
        mixed = (dot(grown[b], stay[0, b]) + dot(grown[1 - b], cross[0, 1 - b])).astype(BF16)
        held[:, cols] = mixed
        sent[:, cols] = dot(mixed, cross[1, b]).astype(BF16)


def first_leaf_step(size, src, leaf, stay, cross, prev, held, sent, token, rows, leaf_in, stay_in, cross_in, sems):
    moves = copies(
        [
            (src.at[pl.ds(0, size)], rows),
            (leaf, leaf_in),
            (stay.at[pl.ds(0, 1)], stay_in),
            (cross.at[pl.ds(0, 2)], cross_in),
        ],
        sems,
    )
    for move in moves:
        move.start()
    for move in moves:
        move.wait()
    leaf_rows(rows, leaf_in, stay_in, cross_in, held, sent, slice(None))
    token[...] = jnp.zeros_like(token)


def leaf_step(start, size, src, leaf, stay, cross, prev, *outs):
    held, sent, token = outs[-3:]
    leaf_rows(src, leaf, stay, cross, held, sent, slice(start, start + size))
    token[...] = jnp.zeros_like(token)


def level_step(level, bounds, extra, held_in, moved, stay, cross, prev, *outs):
    outs = outs[extra:]
    rank = stay.shape[-1]
    count = len(bounds)
    for at, (start, size) in enumerate(bounds):
        held, sent = outs[at], outs[count + at]
        for b in range(2):
            cols = slice(b * rank, (b + 1) * rank)
            mixed = dot(held_in[start : start + size, cols], stay[level, b])
            mixed = (mixed + moved[start : start + size, cols].astype(F32)).astype(BF16)
            held[:, cols] = mixed
            sent[:, cols] = dot(mixed, cross[level + 1, b]).astype(BF16)
    token = outs[-1]
    token[...] = jnp.zeros_like(token)


def last_step(level, start, size, held, moved, stay, out_basis, near, src, rim_a, rim_b, prev, *refs):
    out, token, window, result, sems = refs[-5:]
    rank, points = out_basis.shape[1:]
    rim = rim_a.shape[1]
    blocks = blocks_of(size)
    odd = lax.rem(lax.axis_index("box"), 2) == 1
    leaves = copies([(result.at[pl.ds(at, n)], out.at[pl.ds(start + at, n)]) for at, n in blocks], sems)
    for leave, (at, n) in zip(leaves, blocks):
        part, whole = slice(at, at + n), slice(start + at, start + at + n)
        window[part, :rim] = jnp.where(odd, rim_a[whole], rim_b[whole])
        window[part, rim : rim + 2 * points] = src[whole].astype(BF16)
        window[part, rim + 2 * points :] = jnp.where(odd, rim_b[whole], rim_a[whole])
        for b in range(2):
            cols = slice(b * rank, (b + 1) * rank)
            mixed = (dot(held[part, cols], stay[level, b]) + moved[part, cols].astype(F32)).astype(BF16)
            result[part, b * points : (b + 1) * points] = dot(mixed, out_basis[b]) + dot(
                window[part, b * points : (b + 1) * points + 2 * rim], near[b]
            )
        leave.start()
    for leave in leaves:
        leave.wait()
    token[...] = jnp.zeros_like(token)


def rim_step(src, prev, to_a, to_b, token):
    rim = to_a.shape[1]
    odd = lax.rem(lax.axis_index("box"), 2) == 1
    head, tail = src[:, :rim].astype(BF16), src[:, src.shape[1] - rim :].astype(BF16)
    to_a[...] = jnp.where(odd, head, tail)
    to_b[...] = jnp.where(odd, tail, head)
    token[...] = jnp.zeros_like(token)


ANY = pl.BlockSpec(memory_space=pl.ANY)
VMEM = pl.BlockSpec(memory_space=pltpu.VMEM)
TOKEN = jax.ShapeDtypeStruct((8, 128), F32)
SOME = pl.CostEstimate(flops=6*10**8, bytes_accessed=1, transcendentals=0)
LITTLE = pl.CostEstimate(flops=10**7, bytes_accessed=1, transcendentals=0)


def call(body, operands, in_specs, out_shape, out_specs, scratch, name, mib, aliases=None):
    return pl.pallas_call(
        body,
        in_specs=in_specs,
        out_specs=out_specs,
        out_shape=out_shape,
        scratch_shapes=scratch,
        input_output_aliases=aliases or {},
        compiler_params=pltpu.CompilerParams(vmem_limit_bytes=mib * 1024 * 1024),
        cost_estimate=LITTLE if name in ("last", "near") else SOME,
        name=name,
    )(*operands)


def per_device(sources, leaf_basis, stay_blocks, cross_blocks, out_basis, near_blocks):
    rows, points = sources.shape
    levels, _, rank, _ = stay_blocks.shape
    devices = lax.axis_size("box")
    rim = (near_blocks.shape[1] - near_blocks.shape[2]) // 2
    cuts = [None, cut(rows, FIRST)] + [cut(rows, MIDDLE)] * (levels - 3) + [cut(rows, LAST)]
    order, _ = order_of(cuts, rows)
    pair = lambda size: jax.ShapeDtypeStruct((size, 2 * rank), BF16)
    sems = lambda count: pltpu.SemaphoreType.DMA((count,))
    in_hbm = lambda array: pltpu.with_memory_space_constraint(array, pltpu.HBM)

    token = jnp.zeros(TOKEN.shape, TOKEN.dtype)
    out, rims, taken = None, None, False
    held, moved = {}, {}
    for level, piece in order:
        start, size = piece
        sent = {}
        if level == -2:
            taken = True
            continue
        extra = [*rims] if taken else []
        taken = False
        if level == -1:
            to_a, to_b, token = call(
                rim_step, (sources, token), [VMEM, ANY],
                [jax.ShapeDtypeStruct((rows, rim), BF16)] * 2 + [TOKEN],
                [VMEM] * 3, [], "rims", 8,
            )
            rims = (
                lax.ppermute(to_a, "box", [(i, i ^ 1) for i in range(devices)]),
                lax.ppermute(to_b, "box", [(i, (i - 1 ^ 1) + 1) for i in range(1, devices - 1)]),
            )
        elif level == 0 and start == 0:
            held[1, piece], sent[piece], token = call(
                functools.partial(first_leaf_step, size),
                (*map(in_hbm, (sources, leaf_basis, stay_blocks, cross_blocks)), token),
                [ANY] * 5,
                [pair(size), pair(size), TOKEN],
                [VMEM, VMEM, VMEM],
                [pltpu.VMEM((size, points), F32), pltpu.VMEM(leaf_basis.shape, BF16),
                 pltpu.VMEM((1,) + stay_blocks.shape[1:], BF16), pltpu.VMEM((2,) + cross_blocks.shape[1:], BF16),
                 sems(4)],
                "leaf", 16,
            )
        elif level == 0:
            held[1, piece], sent[piece], token = call(
                functools.partial(leaf_step, start, size),
                (sources, leaf_basis, stay_blocks, cross_blocks, token, *extra),
                [VMEM, VMEM, VMEM, VMEM, ANY] + [ANY] * len(extra),
                [pair(size), pair(size), TOKEN],
                [VMEM, VMEM, VMEM],
                [],
                "leaf", 16,
            )
        elif level < levels - 1:
            children = inside(piece, cuts[level + 1])
            results = call(
                functools.partial(level_step, level, [(q[0] - start, q[1]) for q in children], len(extra)),
                (held.pop((level, piece)), moved.pop((level, piece)), stay_blocks, cross_blocks, token, *extra),
                [VMEM, VMEM, VMEM, VMEM, ANY] + [ANY] * len(extra),
                [pair(q[1]) for q in children] * 2 + [TOKEN],
                [VMEM] * (2 * len(children) + 1),
                [], "near" if level == levels - 2 else "level", 16,
            )
            token = results[-1]
            for which, q in enumerate(children):
                held[level + 1, q] = results[which]
                sent[q] = results[len(children) + which]
        else:
            operands = [held.pop((level, piece)), moved.pop((level, piece)), stay_blocks, out_basis, near_blocks,
                        sources, *rims, token]
            in_specs = [VMEM] * 8 + [ANY]
            aliases = {}
            if out is not None:
                operands.append(out)
                in_specs.append(ANY)
                aliases = {9: 0}
            out, token = call(
                functools.partial(last_step, level, start, size),
                operands, in_specs,
                [jax.ShapeDtypeStruct((rows, points), F32), TOKEN],
                [pl.BlockSpec(memory_space=pltpu.HBM), VMEM],
                [pltpu.VMEM((size, points + 2 * rim), BF16), pltpu.VMEM((size, points), F32),
                 sems(len(blocks_of(size)))],
                "last", 16, aliases,
            )
        for q, array in sent.items():
            moved[level + 1, q] = lax.ppermute(array, "box", [(i, i ^ 1 << level) for i in range(devices)])
    return out


def solution(mesh):
    in_specs = (
        P(None, "box"),
        P("box", None, None),
        P(None, "box", None, None),
        P(None, "box", None, None),
        P("box", None, None),
        P("box", None, None),
    )
    out_specs = P(None, "box")
    return jax.shard_map(
        per_device, mesh=mesh, in_specs=in_specs, out_specs=out_specs, check_vma=False
    )
```

```python
import functools

import jax
import jax.numpy as jnp
from jax import lax
from jax.experimental import pallas as pl
from jax.experimental.pallas import tpu as pltpu
from jax.sharding import PartitionSpec as P

BF16 = jnp.bfloat16
F32 = jnp.float32
SHARES = (12, 17, 20, 22, 23, 20, 14)


def dot(a, b):
    return jnp.dot(a, b, preferred_element_type=F32)


def cut(rows, shares):
    ends = [rows * sum(shares[: at + 1]) // sum(shares) // 16 * 16 for at in range(len(shares))]
    ends[-1] = rows
    starts = [0] + ends[:-1]
    return [(start, end - start) for start, end in zip(starts, ends)]


def order_of(pieces, inward):
    count = len(pieces)
    order = [("leaf", pieces[0]), ("level", pieces[0], 1), ("leaf", pieces[1]), ("swap rims",)]
    for turn in range(2, count + inward + 2):
        new, old = turn - inward, turn - inward - 2
        if turn == inward:
            order.append(("take",))
        if new >= 0 and new != 1:
            order.append(("turn", pieces[new] if new < count else None, pieces[old] if old >= 0 else None))
        for level in range(inward - 1, 0, -1):
            if turn == inward + 1 and level == 1:
                order.append(("take",))
            if 0 <= turn - level < count:
                order.append(("level", pieces[turn - level], level))
        if turn == inward:
            order += [("pass rims",), ("turn", pieces[1], None), ("relay", pieces[new])]
        if turn == inward + 1:
            order.append(("relay", pieces[new]))
        if turn < count:
            order.append(("leaf", pieces[turn]))
        if inward + 1 < turn and new < count:
            order.append(("relay", pieces[new]))
        if old >= 0:
            order.append(("last", pieces[old]))
    return order


def copies(pairs, sems):
    return [pltpu.make_async_copy(src, dst, sems.at[at]) for at, (src, dst) in enumerate(pairs)]


def blocks_of(size):
    step = 128
    return [(at, min(step, size - at)) for at in range(0, size, step)]


def leaf_rows(src, leaf, stay, cross, held, sent, rows):
    points, rank = leaf.shape[1:]
    grown = [
        dot(src[rows, b * points : (b + 1) * points].astype(BF16), leaf[b]).astype(BF16) for b in range(2)
    ]
    for b in range(2):
        cols = slice(b * rank, (b + 1) * rank)
        mixed = (dot(grown[b], stay[0, b]) + dot(grown[1 - b], cross[0, 1 - b])).astype(BF16)
        held[:, cols] = mixed
        sent[:, cols] = dot(mixed, cross[1, b]).astype(BF16)


def first_leaf_step(size, level, src, leaf, stay, cross, prev, held, sent, packed, token, rows, leaf_in, stay_in, cross_in, sems):
    moves = copies(
        [
            *[(src.at[pl.ds(at, n)], rows.at[pl.ds(at, n)]) for at, n in blocks_of(size)],
            (leaf.at[0], leaf_in.at[0]),
            (leaf.at[1], leaf_in.at[1]),
            (stay.at[pl.ds(0, 1)], stay_in),
            (cross.at[pl.ds(0, 2)], cross_in),
            (cross.at[pl.ds(level, 2)], packed.at[pl.ds(0, 2)]),
            (stay.at[pl.ds(level, 2)], packed.at[pl.ds(2, 2)]),
        ],
        sems,
    )
    for move in moves:
        move.start()
    for move in moves[:-2]:
        move.wait()
    leaf_rows(rows, leaf_in, stay_in, cross_in, held, sent, slice(None))
    for move in moves[-2:]:
        move.wait()
    token[...] = jnp.zeros_like(token)


def leaf_step(start, size, src, leaf, stay, cross, prev, *outs):
    held, sent, token = outs[-3:]
    leaf_rows(src, leaf, stay, cross, held, sent, slice(start, start + size))
    token[...] = jnp.zeros_like(token)


def mix(held, moved, block):
    return (dot(held, block) + moved.astype(F32)).astype(BF16)


def level_step(level, held_in, moved, stay, cross, prev, held, sent, token):
    rank = stay.shape[-1]
    for b in range(2):
        cols = slice(b * rank, (b + 1) * rank)
        mixed = mix(held_in[:, cols], moved[:, cols], stay[level, b])
        held[:, cols] = mixed
        sent[:, cols] = dot(mixed, cross[level + 1, b]).astype(BF16)
    token[...] = jnp.zeros_like(token)


def relay_step(level, own, other, stay, cross, theirs_in, prev, own_out, other_out, sent, token):
    rank = stay.shape[-1]
    width = 2 * rank
    size = own.shape[0]
    for b in range(2):
        cols = slice(b * rank, (b + 1) * rank)
        mine, theirs = own[:, cols], other[:size, cols]
        theirs_mixed = (dot(theirs, theirs_in[2, b]) + dot(mine, cross[level, b])).astype(BF16)
        sent[:, cols] = dot(theirs_mixed, theirs_in[1, b]).astype(BF16)
        other_out[:, cols] = theirs_mixed
        mine_mixed = (dot(mine, stay[level, b]) + dot(theirs, theirs_in[0, b])).astype(BF16)
        sent[:, width + b * rank : width + (b + 1) * rank] = dot(mine_mixed, cross[level + 1, b]).astype(BF16)
        own_out[:, cols] = mine_mixed
    token[...] = jnp.zeros_like(token)


def inward_step(level, held_in, moved, stay, prev, held, token):
    rank = stay.shape[-1]
    for b in range(2):
        cols = slice(b * rank, (b + 1) * rank)
        held[:, cols] = mix(held_in[:, cols], moved[:, cols], stay[level, b])
    token[...] = jnp.zeros_like(token)


def turn_step(quarter, level, new, old, *refs):
    refs = list(refs)
    if new:
        held_in, moved = refs.pop(0), refs.pop(0)
    if old:
        own, other, across, theirs_in = (refs.pop(0) for _ in range(4))
    stay, prev = refs.pop(0), refs.pop(0)
    token = refs.pop()
    rank = stay.shape[-1]
    width = 2 * rank
    me = lax.axis_index("box")
    inner = jnp.logical_and(me >= quarter, me < 3 * quarter)
    sent = refs.pop()
    for b in range(2):
        cols = slice(b * rank, (b + 1) * rank)
        shifted = slice(width + b * rank, width + (b + 1) * rank)
        if new:
            going_in = mix(held_in[:, cols], moved[:, cols], stay[level - 2, b])
            refs[0][:, cols] = going_in
        if old:
            refs[-1][:, cols] = mix(own[:, cols], across[:, cols], stay[level, b])
            going_out = mix(other[:, cols], across[:, shifted], theirs_in[3, b])
        if new and old:
            both = min(new, old)
            sent[:both, cols] = jnp.where(inner, going_out[:both], going_in[:both])
            if new > both:
                sent[both:, cols] = going_in[both:]
            if old > both:
                sent[both:, cols] = going_out[both:]
        elif old:
            sent[:, cols] = going_out
    token[...] = jnp.zeros_like(token)


def last_step(quarter, start, size, own, back, out_basis, near, src, rim_a, rim_b, prev, *refs):
    out, token, window, result, sems = refs[-5:]
    rank, points = out_basis.shape[1:]
    rim = rim_a.shape[1]
    blocks = blocks_of(size)
    me = lax.axis_index("box")
    odd = lax.rem(me, 2) == 1
    inner = jnp.logical_and(me >= quarter, me < 3 * quarter)
    leaves = copies([(result.at[pl.ds(at, n)], out.at[pl.ds(start + at, n)]) for at, n in blocks], sems)
    for leave, (at, n) in zip(leaves, blocks):
        part, whole = slice(at, at + n), slice(start + at, start + at + n)
        before, after = jnp.where(odd, rim_a[whole], rim_b[whole]), jnp.where(odd, rim_b[whole], rim_a[whole])
        window[part, :rim] = before
        window[part, rim : rim + 2 * points] = src[whole].astype(BF16)
        window[part, rim + 2 * points :] = after
        for b in range(2):
            cols = slice(b * rank, (b + 1) * rank)
            mixed = jnp.where(inner, own[part, cols], back[part, cols])
            result[part, b * points : (b + 1) * points] = dot(mixed, out_basis[b]) + dot(
                window[part, b * points : (b + 1) * points + 2 * rim], near[b]
            )
        leave.start()
    for leave in leaves:
        leave.wait()
    token[...] = jnp.zeros_like(token)


def rim_step(swap, src, prev, to, token):
    rim = to.shape[1]
    odd = lax.rem(lax.axis_index("box"), 2) == int(swap)
    head, tail = src[:, :rim].astype(BF16), src[:, src.shape[1] - rim :].astype(BF16)
    to[...] = jnp.where(odd, head, tail)
    token[...] = jnp.zeros_like(token)


def take_step(*refs):
    token = refs[-1]
    token[...] = jnp.zeros_like(token)


ANY = pl.BlockSpec(memory_space=pl.ANY)
VMEM = pl.BlockSpec(memory_space=pltpu.VMEM)
TOKEN = jax.ShapeDtypeStruct((8, 128), F32)
SOME = pl.CostEstimate(flops=3 * 10**9, bytes_accessed=1, transcendentals=0)
LITTLE = pl.CostEstimate(flops=10**7, bytes_accessed=1, transcendentals=0)


LIGHT = ("last", "relay")


def call(body, operands, in_specs, out_shape, out_specs, scratch, name, mib, aliases=None):
    return pl.pallas_call(
        body,
        in_specs=in_specs,
        out_specs=out_specs,
        out_shape=out_shape,
        scratch_shapes=scratch,
        input_output_aliases=aliases or {},
        compiler_params=pltpu.CompilerParams(vmem_limit_bytes=mib * 1024 * 1024),
        cost_estimate=LITTLE if name in LIGHT else SOME,
        name=name,
    )(*operands)


def per_device(sources, leaf_basis, stay_blocks, cross_blocks, out_basis, near_blocks):
    rows, points = sources.shape
    levels, _, rank, _ = stay_blocks.shape
    devices = lax.axis_size("box")
    quarter = devices // 4
    inward = levels - 3
    rim = (near_blocks.shape[1] - near_blocks.shape[2]) // 2
    pieces = cut(rows, SHARES)
    array = lambda *shape: jax.ShapeDtypeStruct(shape, BF16)
    sems = lambda count: pltpu.SemaphoreType.DMA((count,))
    in_hbm = lambda operand: pltpu.with_memory_space_constraint(operand, pltpu.HBM)
    apart = lambda gap: [(i, i ^ gap) for i in range(devices)]
    across = [
        (i, i ^ 3 * quarter if quarter <= i < 3 * quarter else i ^ 1) for i in range(devices)
    ]
    next_over = [(i, (i - 1 ^ 1) + 1) for i in range(1, devices - 1)]
    send = lambda operand, pairs: lax.ppermute(operand, "box", pairs)
    small = tuple(stay_blocks.shape[1:])

    token = jnp.zeros(TOKEN.shape, TOKEN.dtype)
    out, rim_a, rim_b, waiting, theirs = (None,) * 5
    held, moved, kept, across_in, swapped = {}, {}, {}, {}, {}
    for step, *rest in order_of(pieces, inward):
        piece = rest[0] if rest else None
        start, size = piece or (0, rows)
        pair = array(size, 2 * rank)
        if step == "leaf" and start == 0:
            held[1, piece], sent, packed, token = call(
                functools.partial(first_leaf_step, size, levels - 2),
                (*map(in_hbm, (sources, leaf_basis, stay_blocks, cross_blocks)), token),
                [ANY] * 5, [pair, pair, array(4, *small), TOKEN], [VMEM] * 4,
                [pltpu.VMEM((size, points), F32), pltpu.VMEM(leaf_basis.shape, BF16),
                 pltpu.VMEM((1,) + small, BF16), pltpu.VMEM((2,) + small, BF16), sems(6 + len(blocks_of(size)))],
                "leaf", 16,
            )
            moved[1, piece] = send(sent, apart(1))
            theirs = send(packed, apart(quarter))
        elif step == "leaf":
            held[1, piece], sent, token = call(
                functools.partial(leaf_step, start, size),
                (sources, leaf_basis, stay_blocks, cross_blocks, token),
                [VMEM] * 4 + [ANY], [pair, pair, TOKEN], [VMEM] * 3, [], "leaf", 16,
            )
            moved[1, piece] = send(sent, apart(1))
        elif step == "level":
            level = rest[1]
            held[level + 1, piece], sent, token = call(
                functools.partial(level_step, level),
                (held.pop((level, piece)), moved.pop((level, piece)), stay_blocks, cross_blocks, token),
                [VMEM] * 4 + [ANY], [pair, pair, TOKEN], [VMEM] * 3, [], "level", 16,
            )
            moved[level + 1, piece] = send(sent, apart(1 << level))
        elif step == "turn":
            old = rest[1]
            operands, results = (), []
            if piece:
                operands += held.pop((inward, piece)), moved.pop((inward, piece))
                results.append(pair)
            if old:
                operands += (*kept.pop(old), across_in.pop(old), theirs)
                results.append(array(old[1], 2 * rank))
            if old or not piece:
                results.append(array(max(size if piece else 0, old[1]), 2 * rank))
            *results, token = call(
                functools.partial(turn_step, quarter, levels - 1, size if piece else 0, old[1] if old else 0)
                if old else functools.partial(inward_step, levels - 3),
                (*operands, stay_blocks, token),
                [VMEM] * (len(operands) + 1) + [ANY], results + [TOKEN], [VMEM] * (len(results) + 1), [], "turn", 16,
            )
            message = send(results[-1], apart(quarter))
            if piece:
                swapped[piece] = results[0], message
            if old:
                kept[old] = results[-2], message
        elif step == "relay":
            own, arrived = swapped.pop(piece)
            own, other, sent, token = call(
                functools.partial(relay_step, levels - 2),
                (own, arrived, stay_blocks, cross_blocks, theirs, token),
                [VMEM] * 5 + [ANY], [pair, pair, array(size, 4 * rank), TOKEN], [VMEM] * 4, [], "relay", 16,
            )
            kept[piece] = own, other
            across_in[piece] = send(sent, across)
        elif step == "last":
            operands = [*kept.pop(piece), out_basis, near_blocks, sources, rim_a, rim_b, token]
            in_specs = [VMEM] * 7 + [ANY]
            aliases = {}
            if out is not None:
                operands.append(out)
                in_specs.append(ANY)
                aliases = {8: 0}
            out, token = call(
                functools.partial(last_step, quarter, start, size),
                operands, in_specs,
                [jax.ShapeDtypeStruct((rows, points), F32), TOKEN],
                [pl.BlockSpec(memory_space=pltpu.HBM), VMEM],
                [pltpu.VMEM((size, points + 2 * rim), BF16), pltpu.VMEM((size, points), F32),
                 sems(len(blocks_of(size)))],
                "last", 16, aliases,
            )
        elif step == "take":
            (token,) = call(take_step, (waiting, token), [ANY] * 2, [TOKEN], [VMEM], [], "take", 8)
        else:
            swap = step == "swap rims"
            to, token = call(
                functools.partial(rim_step, swap), (sources, token), [VMEM, ANY], [array(rows, rim), TOKEN],
                [VMEM] * 2, [], "rims", 8,
            )
            waiting = send(to, apart(1) if swap else next_over)
            rim_a, rim_b = (waiting, None) if swap else (rim_a, waiting)
    return out


def solution(mesh):
    in_specs = (
        P(None, "box"),
        P("box", None, None),
        P(None, "box", None, None),
        P(None, "box", None, None),
        P("box", None, None),
        P("box", None, None),
    )
    out_specs = P(None, "box")
    return jax.shard_map(
        per_device, mesh=mesh, in_specs=in_specs, out_specs=out_specs, check_vma=False
    )
```

```python
import functools

import jax
import jax.numpy as jnp
from jax import lax
from jax.experimental import pallas as pl
from jax.experimental.pallas import tpu as pltpu
from jax.sharding import PartitionSpec as P

BF16 = jnp.bfloat16
F32 = jnp.float32
SHARES = (13, 18, 20, 22, 23, 21, 11)


def dot(a, b):
    return jnp.dot(a, b, preferred_element_type=F32)


def cut(rows, shares):
    ends = [rows * sum(shares[: at + 1]) // sum(shares) // 16 * 16 for at in range(len(shares))]
    ends[-1] = rows
    starts = [0] + ends[:-1]
    return [(start, end - start) for start, end in zip(starts, ends)]


def order_of(pieces, inward):
    count = len(pieces)
    order = [("leaf", pieces[0]), ("level", pieces[0], 1), ("leaf", pieces[1]), ("rims", "chip")]
    arrived, landed = [], []
    for turn in range(2, count + inward + 2):
        new, old = turn - inward, turn - inward - 2
        if turn == inward:
            order.append(("take", "chip"))
        if turn == inward:
            order.append(("rims", "middle"))
        if new >= 0 and new != 1:
            order.append(("turn", pieces[new] if new < count else None, pieces[old] if old >= 0 else None))
        if turn > count:
            order += [("take", "next")] if turn == count + 1 else []
            order += [("last", piece) for piece in arrived]
            arrived = []
        for level in range(inward - 1, 0, -1):
            if turn == inward + 1 and level == 1:
                order.append(("take", "middle"))
            if 0 <= turn - level < count:
                order.append(("level", pieces[turn - level], level))
        if turn == inward:
            order += [("turn", pieces[1], None), ("relay", pieces[new])]
        if turn == inward + 1:
            order.append(("relay", pieces[new]))
        if turn < count:
            order.append(("leaf", pieces[turn]))
        if turn == count:
            order.append(("rims", "next"))
        if inward + 1 < turn and new < count:
            order.append(("relay", pieces[new]))
        if old >= 0:
            arrived.append(pieces[old])
    return order + [("last", piece) for piece in arrived]


def copies(pairs, sems):
    return [pltpu.make_async_copy(src, dst, sems.at[at]) for at, (src, dst) in enumerate(pairs)]


def blocks_of(size):
    step = 128
    return [(at, min(step, size - at)) for at in range(0, size, step)]


def leaf_rows(src, leaf, stay, cross, held, sent, rows):
    points, rank = leaf.shape[1:]
    grown = [
        dot(src[rows, b * points : (b + 1) * points].astype(BF16), leaf[b]).astype(BF16) for b in range(2)
    ]
    for b in range(2):
        cols = slice(b * rank, (b + 1) * rank)
        mixed = (dot(grown[b], stay[0, b]) + dot(grown[1 - b], cross[0, 1 - b])).astype(BF16)
        held[:, cols] = mixed
        sent[:, cols] = dot(mixed, cross[1, b]).astype(BF16)


def first_leaf_step(size, level, src, leaf, stay, cross, prev, held, sent, packed, token, rows, leaf_in, stay_in, cross_in, sems):
    moves = copies(
        [
            *[(src.at[pl.ds(at, n)], rows.at[pl.ds(at, n)]) for at, n in blocks_of(size)],
            (leaf.at[0], leaf_in.at[0]),
            (leaf.at[1], leaf_in.at[1]),
            (stay.at[pl.ds(0, 1)], stay_in),
            (cross.at[pl.ds(0, 2)], cross_in),
            (cross.at[pl.ds(level, 2)], packed.at[pl.ds(0, 2)]),
            (stay.at[pl.ds(level, 2)], packed.at[pl.ds(2, 2)]),
        ],
        sems,
    )
    for move in moves:
        move.start()
    for move in moves[:-2]:
        move.wait()
    leaf_rows(rows, leaf_in, stay_in, cross_in, held, sent, slice(None))
    for move in moves[-2:]:
        move.wait()
    token[...] = jnp.zeros_like(token)


def leaf_step(start, size, src, leaf, stay, cross, prev, *outs):
    held, sent, token = outs[-3:]
    leaf_rows(src, leaf, stay, cross, held, sent, slice(start, start + size))
    token[...] = jnp.zeros_like(token)


def mix(held, moved, block):
    return (dot(held, block) + moved.astype(F32)).astype(BF16)


def level_step(level, held_in, moved, stay, cross, prev, held, sent, token):
    rank = stay.shape[-1]
    for b in range(2):
        cols = slice(b * rank, (b + 1) * rank)
        mixed = mix(held_in[:, cols], moved[:, cols], stay[level, b])
        held[:, cols] = mixed
        sent[:, cols] = dot(mixed, cross[level + 1, b]).astype(BF16)
    token[...] = jnp.zeros_like(token)


def relay_step(level, own, other, stay, cross, theirs_in, prev, own_out, other_out, sent, token):
    rank = stay.shape[-1]
    width = 2 * rank
    size = own.shape[0]
    for b in range(2):
        cols = slice(b * rank, (b + 1) * rank)
        mine, theirs = own[:, cols], other[:size, cols]
        theirs_mixed = (dot(theirs, theirs_in[2, b]) + dot(mine, cross[level, b])).astype(BF16)
        sent[:, cols] = dot(theirs_mixed, theirs_in[1, b]).astype(BF16)
        other_out[:, cols] = theirs_mixed
        mine_mixed = (dot(mine, stay[level, b]) + dot(theirs, theirs_in[0, b])).astype(BF16)
        sent[:, width + b * rank : width + (b + 1) * rank] = dot(mine_mixed, cross[level + 1, b]).astype(BF16)
        own_out[:, cols] = mine_mixed
    token[...] = jnp.zeros_like(token)


def inward_step(level, held_in, moved, stay, prev, held, token):
    rank = stay.shape[-1]
    for b in range(2):
        cols = slice(b * rank, (b + 1) * rank)
        held[:, cols] = mix(held_in[:, cols], moved[:, cols], stay[level, b])
    token[...] = jnp.zeros_like(token)


def turn_step(quarter, level, new, old, *refs):
    refs = list(refs)
    if new:
        held_in, moved = refs.pop(0), refs.pop(0)
    if old:
        own, other, across, theirs_in = (refs.pop(0) for _ in range(4))
    stay, prev = refs.pop(0), refs.pop(0)
    token = refs.pop()
    rank = stay.shape[-1]
    width = 2 * rank
    me = lax.axis_index("box")
    inner = jnp.logical_and(me >= quarter, me < 3 * quarter)
    sent = refs.pop()
    for b in range(2):
        cols = slice(b * rank, (b + 1) * rank)
        shifted = slice(width + b * rank, width + (b + 1) * rank)
        if new:
            going_in = mix(held_in[:, cols], moved[:, cols], stay[level - 2, b])
            refs[0][:, cols] = going_in
        if old:
            refs[-1][:, cols] = mix(own[:, cols], across[:, cols], stay[level, b])
            going_out = mix(other[:, cols], across[:, shifted], theirs_in[3, b])
        if new and old:
            both = min(new, old)
            sent[:both, cols] = jnp.where(inner, going_out[:both], going_in[:both])
            if new > both:
                sent[both:, cols] = going_in[both:]
            if old > both:
                sent[both:, cols] = going_out[both:]
        elif old:
            sent[:, cols] = going_out
    token[...] = jnp.zeros_like(token)


def last_step(quarter, start, size, own, back, out_basis, near, src, rim_a, rim_m, rim_n, prev, *refs):
    out, token, window, result, sems = refs[-5:]
    rank, points = out_basis.shape[1:]
    rim = rim_a.shape[1]
    blocks = blocks_of(size)
    me = lax.axis_index("box")
    odd = lax.rem(me, 2) == 1
    inner = jnp.logical_and(me >= quarter, me < 3 * quarter)
    halfway = jnp.logical_or(me == 2 * quarter - 1, me == 2 * quarter)
    leaves = copies([(result.at[pl.ds(at, n)], out.at[pl.ds(start + at, n)]) for at, n in blocks], sems)
    for leave, (at, n) in zip(leaves, blocks):
        part, whole = slice(at, at + n), slice(start + at, start + at + n)
        rim_b = jnp.where(halfway, rim_m[whole], rim_n[whole])
        before, after = jnp.where(odd, rim_a[whole], rim_b), jnp.where(odd, rim_b, rim_a[whole])
        window[part, :rim] = before
        window[part, rim : rim + 2 * points] = src[whole].astype(BF16)
        window[part, rim + 2 * points :] = after
        for b in range(2):
            cols = slice(b * rank, (b + 1) * rank)
            mixed = jnp.where(inner, own[part, cols], back[part, cols])
            result[part, b * points : (b + 1) * points] = dot(mixed, out_basis[b]) + dot(
                window[part, b * points : (b + 1) * points + 2 * rim], near[b]
            )
        leave.start()
    for leave in leaves:
        leave.wait()
    token[...] = jnp.zeros_like(token)


def rim_step(swap, src, prev, to, token):
    rim = to.shape[1]
    odd = lax.rem(lax.axis_index("box"), 2) == int(swap)
    head, tail = src[:, :rim].astype(BF16), src[:, src.shape[1] - rim :].astype(BF16)
    to[...] = jnp.where(odd, head, tail)
    token[...] = jnp.zeros_like(token)


def take_step(*refs):
    token = refs[-1]
    token[...] = jnp.zeros_like(token)


ANY = pl.BlockSpec(memory_space=pl.ANY)
VMEM = pl.BlockSpec(memory_space=pltpu.VMEM)
TOKEN = jax.ShapeDtypeStruct((8, 128), F32)
SOME = pl.CostEstimate(flops=3 * 10**9, bytes_accessed=1, transcendentals=0)
LITTLE = pl.CostEstimate(flops=10**7, bytes_accessed=1, transcendentals=0)


LIGHT = ("last", "relay")


def call(body, operands, in_specs, out_shape, out_specs, scratch, name, mib, aliases=None):
    return pl.pallas_call(
        body,
        in_specs=in_specs,
        out_specs=out_specs,
        out_shape=out_shape,
        scratch_shapes=scratch,
        input_output_aliases=aliases or {},
        compiler_params=pltpu.CompilerParams(vmem_limit_bytes=mib * 1024 * 1024),
        cost_estimate=LITTLE if name in LIGHT else SOME,
        name=name,
    )(*operands)


def per_device(sources, leaf_basis, stay_blocks, cross_blocks, out_basis, near_blocks):
    rows, points = sources.shape
    levels, _, rank, _ = stay_blocks.shape
    devices = lax.axis_size("box")
    quarter = devices // 4
    inward = levels - 3
    rim = (near_blocks.shape[1] - near_blocks.shape[2]) // 2
    pieces = cut(rows, SHARES)
    array = lambda *shape: jax.ShapeDtypeStruct(shape, BF16)
    sems = lambda count: pltpu.SemaphoreType.DMA((count,))
    in_hbm = lambda operand: pltpu.with_memory_space_constraint(operand, pltpu.HBM)
    apart = lambda gap: [(i, i ^ gap) for i in range(devices)]
    across = [
        (i, i ^ 3 * quarter if quarter <= i < 3 * quarter else i ^ 1) for i in range(devices)
    ]
    middle = [(devices // 2 - 1, devices // 2), (devices // 2, devices // 2 - 1)]
    next_over = [(i, (i - 1 ^ 1) + 1) for i in range(1, devices - 1)]
    next_over = [link for link in next_over if link not in middle]
    send = lambda operand, pairs: lax.ppermute(operand, "box", pairs)
    small = tuple(stay_blocks.shape[1:])

    token = jnp.zeros(TOKEN.shape, TOKEN.dtype)
    out, theirs = None, None
    held, moved, kept, across_in, swapped, rims = {}, {}, {}, {}, {}, {}
    for step, *rest in order_of(pieces, inward):
        piece = rest[0] if rest else None
        start, size = piece if isinstance(piece, tuple) else (0, rows)
        pair = array(size, 2 * rank)
        if step == "leaf" and start == 0:
            held[1, piece], sent, packed, token = call(
                functools.partial(first_leaf_step, size, levels - 2),
                (*map(in_hbm, (sources, leaf_basis, stay_blocks, cross_blocks)), token),
                [ANY] * 5, [pair, pair, array(4, *small), TOKEN], [VMEM] * 4,
                [pltpu.VMEM((size, points), F32), pltpu.VMEM(leaf_basis.shape, BF16),
                 pltpu.VMEM((1,) + small, BF16), pltpu.VMEM((2,) + small, BF16), sems(6 + len(blocks_of(size)))],
                "leaf", 16,
            )
            moved[1, piece] = send(sent, apart(1))
            theirs = send(packed, apart(quarter))
        elif step == "leaf":
            held[1, piece], sent, token = call(
                functools.partial(leaf_step, start, size),
                (sources, leaf_basis, stay_blocks, cross_blocks, token),
                [VMEM] * 4 + [ANY], [pair, pair, TOKEN], [VMEM] * 3, [], "leaf", 16,
            )
            moved[1, piece] = send(sent, apart(1))
        elif step == "level":
            level = rest[1]
            held[level + 1, piece], sent, token = call(
                functools.partial(level_step, level),
                (held.pop((level, piece)), moved.pop((level, piece)), stay_blocks, cross_blocks, token),
                [VMEM] * 4 + [ANY], [pair, pair, TOKEN], [VMEM] * 3, [], "level", 16,
            )
            moved[level + 1, piece] = send(sent, apart(1 << level))
        elif step == "turn":
            old = rest[1]
            operands, results = (), []
            if piece:
                operands += held.pop((inward, piece)), moved.pop((inward, piece))
                results.append(pair)
            if old:
                operands += (*kept.pop(old), across_in.pop(old), theirs)
                results.append(array(old[1], 2 * rank))
            if old or not piece:
                results.append(array(max(size if piece else 0, old[1]), 2 * rank))
            *results, token = call(
                functools.partial(turn_step, quarter, levels - 1, size if piece else 0, old[1] if old else 0)
                if old else functools.partial(inward_step, levels - 3),
                (*operands, stay_blocks, token),
                [VMEM] * (len(operands) + 1) + [ANY], results + [TOKEN], [VMEM] * (len(results) + 1), [], "turn", 16,
            )
            message = send(results[-1], apart(quarter))
            if piece:
                swapped[piece] = results[0], message
            if old:
                kept[old] = results[-2], message
        elif step == "relay":
            own, arrived = swapped.pop(piece)
            own, other, sent, token = call(
                functools.partial(relay_step, levels - 2),
                (own, arrived, stay_blocks, cross_blocks, theirs, token),
                [VMEM] * 5 + [ANY], [pair, pair, array(size, 4 * rank), TOKEN], [VMEM] * 4, [], "relay", 16,
            )
            kept[piece] = own, other
            across_in[piece] = send(sent, across)
        elif step == "last":
            operands = [*kept.pop(piece), out_basis, near_blocks, sources, rims["chip"], rims["middle"],
                        rims["next"], token]
            in_specs = [VMEM] * 8 + [ANY]
            aliases = {}
            if out is not None:
                operands.append(out)
                in_specs.append(ANY)
                aliases = {9: 0}
            out, token = call(
                functools.partial(last_step, quarter, start, size),
                operands, in_specs,
                [jax.ShapeDtypeStruct((rows, points), F32), TOKEN],
                [pl.BlockSpec(memory_space=pltpu.HBM), VMEM],
                [pltpu.VMEM((size, points + 2 * rim), BF16), pltpu.VMEM((size, points), F32),
                 sems(len(blocks_of(size)))],
                "last", 16, aliases,
            )
        elif step == "take":
            (token,) = call(take_step, (rims[piece], token), [ANY] * 2, [TOKEN], [VMEM], [], "take", 8)
        else:
            to, token = call(
                functools.partial(rim_step, piece == "chip"), (sources, token), [VMEM, ANY],
                [array(rows, rim), TOKEN], [VMEM] * 2, [], "rims", 8,
            )
            rims[piece] = send(to, {"chip": apart(1), "middle": middle, "next": next_over}[piece])
    return out


def solution(mesh):
    in_specs = (
        P(None, "box"),
        P("box", None, None),
        P(None, "box", None, None),
        P(None, "box", None, None),
        P("box", None, None),
        P("box", None, None),
    )
    out_specs = P(None, "box")
    return jax.shard_map(
        per_device, mesh=mesh, in_specs=in_specs, out_specs=out_specs, check_vma=False
    )
```

```python
import functools

import jax
import jax.numpy as jnp
from jax import lax
from jax.experimental import pallas as pl
from jax.experimental.pallas import tpu as pltpu
from jax.sharding import PartitionSpec as P

BF16 = jnp.bfloat16
F32 = jnp.float32
SHARES = (15, 21, 25, 28, 25, 14)


def dot(a, b):
    return jnp.dot(a, b, preferred_element_type=F32)


def cut(rows, shares):
    ends = [rows * sum(shares[: at + 1]) // sum(shares) // 16 * 16 for at in range(len(shares))]
    ends[-1] = rows
    starts = [0] + ends[:-1]
    return [(start, end - start) for start, end in zip(starts, ends)]


def order_of(pieces, inward):
    count = len(pieces)
    order = [("leaf", pieces[0]), ("level", pieces[0], 1), ("leaf", pieces[1]), ("rims", "chip")]
    arrived, landed = [], []
    for turn in range(2, count + inward + 2):
        new, old = turn - inward, turn - inward - 2
        if turn == inward:
            order.append(("take", "chip"))
        if new >= 0 and new != 1:
            order.append(("turn", pieces[new] if new < count else None, pieces[old] if old >= 0 else None))
        if turn > count:
            order += [("take", "next")] if turn == count + 1 else []
            order += [("last", piece) for piece in arrived]
            arrived = []
        for level in range(inward - 1, 0, -1):
            if turn == inward + 1 and level == 1:
                order.append(("take", "middle"))
            if 0 <= turn - level < count:
                order.append(("level", pieces[turn - level], level))
        if turn == inward:
            order += [("rims", "middle"), ("turn", pieces[1], None), ("relay", pieces[new])]
        if turn == inward + 1:
            order.append(("relay", pieces[new]))
        if turn < count:
            order.append(("leaf", pieces[turn]))
        if turn == count:
            order.append(("rims", "next"))
        if inward + 1 < turn and new < count:
            order.append(("relay", pieces[new]))
        if old >= 0:
            arrived.append(pieces[old])
    return order + [("last", piece) for piece in arrived]


def copies(pairs, sems):
    return [pltpu.make_async_copy(src, dst, sems.at[at]) for at, (src, dst) in enumerate(pairs)]


def blocks_of(size):
    step = 128
    return [(at, min(step, size - at)) for at in range(0, size, step)]


def leaf_rows(src, leaf, stay, cross, held, sent, rows):
    points, rank = leaf.shape[1:]
    grown = [
        dot(src[rows, b * points : (b + 1) * points].astype(BF16), leaf[b]).astype(BF16) for b in range(2)
    ]
    for b in range(2):
        cols = slice(b * rank, (b + 1) * rank)
        mixed = (dot(grown[b], stay[0, b]) + dot(grown[1 - b], cross[0, 1 - b])).astype(BF16)
        held[:, cols] = mixed
        sent[:, cols] = dot(mixed, cross[1, b]).astype(BF16)


def first_leaf_step(size, level, src, leaf, stay, cross, prev, held, sent, packed, token, rows, leaf_in, stay_in, cross_in, sems):
    moves = copies(
        [
            *[(src.at[pl.ds(at, n)], rows.at[pl.ds(at, n)]) for at, n in blocks_of(size)],
            (leaf.at[0], leaf_in.at[0]),
            (leaf.at[1], leaf_in.at[1]),
            (stay.at[pl.ds(0, 1)], stay_in),
            (cross.at[pl.ds(0, 2)], cross_in),
            (cross.at[pl.ds(level, 2)], packed.at[pl.ds(0, 2)]),
            (stay.at[pl.ds(level, 2)], packed.at[pl.ds(2, 2)]),
        ],
        sems,
    )
    for move in moves:
        move.start()
    for move in moves[:-2]:
        move.wait()
    leaf_rows(rows, leaf_in, stay_in, cross_in, held, sent, slice(None))
    for move in moves[-2:]:
        move.wait()
    token[...] = jnp.zeros_like(token)


def leaf_step(start, size, src, leaf, stay, cross, prev, *outs):
    held, sent, token = outs[-3:]
    leaf_rows(src, leaf, stay, cross, held, sent, slice(start, start + size))
    token[...] = jnp.zeros_like(token)


def mix(held, moved, block):
    return (dot(held, block) + moved.astype(F32)).astype(BF16)


def level_step(level, held_in, moved, stay, cross, prev, held, sent, token):
    rank = stay.shape[-1]
    for b in range(2):
        cols = slice(b * rank, (b + 1) * rank)
        mixed = mix(held_in[:, cols], moved[:, cols], stay[level, b])
        held[:, cols] = mixed
        sent[:, cols] = dot(mixed, cross[level + 1, b]).astype(BF16)
    token[...] = jnp.zeros_like(token)


def relay_step(level, own, other, stay, cross, theirs_in, prev, own_out, other_out, sent, token):
    rank = stay.shape[-1]
    width = 2 * rank
    size = own.shape[0]
    for b in range(2):
        cols = slice(b * rank, (b + 1) * rank)
        mine, theirs = own[:, cols], other[:size, cols]
        theirs_mixed = (dot(theirs, theirs_in[2, b]) + dot(mine, cross[level, b])).astype(BF16)
        sent[:, cols] = dot(theirs_mixed, theirs_in[1, b]).astype(BF16)
        other_out[:, cols] = theirs_mixed
        mine_mixed = (dot(mine, stay[level, b]) + dot(theirs, theirs_in[0, b])).astype(BF16)
        sent[:, width + b * rank : width + (b + 1) * rank] = dot(mine_mixed, cross[level + 1, b]).astype(BF16)
        own_out[:, cols] = mine_mixed
    token[...] = jnp.zeros_like(token)


def inward_step(level, held_in, moved, stay, prev, held, token):
    rank = stay.shape[-1]
    for b in range(2):
        cols = slice(b * rank, (b + 1) * rank)
        held[:, cols] = mix(held_in[:, cols], moved[:, cols], stay[level, b])
    token[...] = jnp.zeros_like(token)


def turn_step(quarter, level, new, old, *refs):
    refs = list(refs)
    if new:
        held_in, moved = refs.pop(0), refs.pop(0)
    if old:
        own, other, across, theirs_in = (refs.pop(0) for _ in range(4))
    stay, prev = refs.pop(0), refs.pop(0)
    token = refs.pop()
    rank = stay.shape[-1]
    width = 2 * rank
    me = lax.axis_index("box")
    inner = jnp.logical_and(me >= quarter, me < 3 * quarter)
    sent = refs.pop()
    for b in range(2):
        cols = slice(b * rank, (b + 1) * rank)
        shifted = slice(width + b * rank, width + (b + 1) * rank)
        if new:
            going_in = mix(held_in[:, cols], moved[:, cols], stay[level - 2, b])
            refs[0][:, cols] = going_in
        if old:
            refs[-1][:, cols] = mix(own[:, cols], across[:, cols], stay[level, b])
            going_out = mix(other[:, cols], across[:, shifted], theirs_in[3, b])
        if new and old:
            both = min(new, old)
            sent[:both, cols] = jnp.where(inner, going_out[:both], going_in[:both])
            if new > both:
                sent[both:, cols] = going_in[both:]
            if old > both:
                sent[both:, cols] = going_out[both:]
        elif old:
            sent[:, cols] = going_out
    token[...] = jnp.zeros_like(token)


def last_step(quarter, start, size, own, back, out_basis, near, src, rim_a, rim_m, rim_n, prev, *refs):
    out, token, window, result, sems = refs[-5:]
    rank, points = out_basis.shape[1:]
    rim = rim_a.shape[1]
    blocks = blocks_of(size)
    me = lax.axis_index("box")
    odd = lax.rem(me, 2) == 1
    inner = jnp.logical_and(me >= quarter, me < 3 * quarter)
    halfway = jnp.logical_or(me == 2 * quarter - 1, me == 2 * quarter)
    leaves = copies([(result.at[pl.ds(at, n)], out.at[pl.ds(start + at, n)]) for at, n in blocks], sems)
    for leave, (at, n) in zip(leaves, blocks):
        part, whole = slice(at, at + n), slice(start + at, start + at + n)
        rim_b = jnp.where(halfway, rim_m[whole], rim_n[whole])
        before, after = jnp.where(odd, rim_a[whole], rim_b), jnp.where(odd, rim_b, rim_a[whole])
        window[part, :rim] = before
        window[part, rim : rim + 2 * points] = src[whole].astype(BF16)
        window[part, rim + 2 * points :] = after
        for b in range(2):
            cols = slice(b * rank, (b + 1) * rank)
            mixed = jnp.where(inner, own[part, cols], back[part, cols])
            result[part, b * points : (b + 1) * points] = dot(mixed, out_basis[b]) + dot(
                window[part, b * points : (b + 1) * points + 2 * rim], near[b]
            )
        leave.start()
    for leave in leaves:
        leave.wait()
    token[...] = jnp.zeros_like(token)


def rim_step(swap, src, prev, to, token):
    rim = to.shape[1]
    odd = lax.rem(lax.axis_index("box"), 2) == int(swap)
    head, tail = src[:, :rim].astype(BF16), src[:, src.shape[1] - rim :].astype(BF16)
    to[...] = jnp.where(odd, head, tail)
    token[...] = jnp.zeros_like(token)


def take_step(*refs):
    token = refs[-1]
    token[...] = jnp.zeros_like(token)


ANY = pl.BlockSpec(memory_space=pl.ANY)
VMEM = pl.BlockSpec(memory_space=pltpu.VMEM)
TOKEN = jax.ShapeDtypeStruct((8, 128), F32)
SOME = pl.CostEstimate(flops=3 * 10**9, bytes_accessed=1, transcendentals=0)
LITTLE = pl.CostEstimate(flops=10**7, bytes_accessed=1, transcendentals=0)


LIGHT = ("last", "relay")


def call(body, operands, in_specs, out_shape, out_specs, scratch, name, mib, aliases=None):
    return pl.pallas_call(
        body,
        in_specs=in_specs,
        out_specs=out_specs,
        out_shape=out_shape,
        scratch_shapes=scratch,
        input_output_aliases=aliases or {},
        compiler_params=pltpu.CompilerParams(vmem_limit_bytes=mib * 1024 * 1024),
        cost_estimate=LITTLE if name in LIGHT else SOME,
        name=name,
    )(*operands)


def per_device(sources, leaf_basis, stay_blocks, cross_blocks, out_basis, near_blocks):
    rows, points = sources.shape
    levels, _, rank, _ = stay_blocks.shape
    devices = lax.axis_size("box")
    quarter = devices // 4
    inward = levels - 3
    rim = (near_blocks.shape[1] - near_blocks.shape[2]) // 2
    pieces = cut(rows, SHARES)
    array = lambda *shape: jax.ShapeDtypeStruct(shape, BF16)
    sems = lambda count: pltpu.SemaphoreType.DMA((count,))
    in_hbm = lambda operand: pltpu.with_memory_space_constraint(operand, pltpu.HBM)
    apart = lambda gap: [(i, i ^ gap) for i in range(devices)]
    across = [
        (i, i ^ 3 * quarter if quarter <= i < 3 * quarter else i ^ 1) for i in range(devices)
    ]
    middle = [(devices // 2 - 1, devices // 2), (devices // 2, devices // 2 - 1)]
    next_over = [(i, (i - 1 ^ 1) + 1) for i in range(1, devices - 1)]
    next_over = [link for link in next_over if link not in middle]
    send = lambda operand, pairs: lax.ppermute(operand, "box", pairs)
    small = tuple(stay_blocks.shape[1:])

    token = jnp.zeros(TOKEN.shape, TOKEN.dtype)
    out, theirs = None, None
    held, moved, kept, across_in, swapped, rims = {}, {}, {}, {}, {}, {}
    for step, *rest in order_of(pieces, inward):
        piece = rest[0] if rest else None
        start, size = piece if isinstance(piece, tuple) else (0, rows)
        pair = array(size, 2 * rank)
        if step == "leaf" and start == 0:
            held[1, piece], sent, packed, token = call(
                functools.partial(first_leaf_step, size, levels - 2),
                (*map(in_hbm, (sources, leaf_basis, stay_blocks, cross_blocks)), token),
                [ANY] * 5, [pair, pair, array(4, *small), TOKEN], [VMEM] * 4,
                [pltpu.VMEM((size, points), F32), pltpu.VMEM(leaf_basis.shape, BF16),
                 pltpu.VMEM((1,) + small, BF16), pltpu.VMEM((2,) + small, BF16), sems(6 + len(blocks_of(size)))],
                "leaf", 16,
            )
            moved[1, piece] = send(sent, apart(1))
            theirs = send(packed, apart(quarter))
        elif step == "leaf":
            held[1, piece], sent, token = call(
                functools.partial(leaf_step, start, size),
                (sources, leaf_basis, stay_blocks, cross_blocks, token),
                [VMEM] * 4 + [ANY], [pair, pair, TOKEN], [VMEM] * 3, [], "leaf", 16,
            )
            moved[1, piece] = send(sent, apart(1))
        elif step == "level":
            level = rest[1]
            held[level + 1, piece], sent, token = call(
                functools.partial(level_step, level),
                (held.pop((level, piece)), moved.pop((level, piece)), stay_blocks, cross_blocks, token),
                [VMEM] * 4 + [ANY], [pair, pair, TOKEN], [VMEM] * 3, [], "level", 16,
            )
            moved[level + 1, piece] = send(sent, apart(1 << level))
        elif step == "turn":
            old = rest[1]
            operands, results = (), []
            if piece:
                operands += held.pop((inward, piece)), moved.pop((inward, piece))
                results.append(pair)
            if old:
                operands += (*kept.pop(old), across_in.pop(old), theirs)
                results.append(array(old[1], 2 * rank))
            if old or not piece:
                results.append(array(max(size if piece else 0, old[1]), 2 * rank))
            *results, token = call(
                functools.partial(turn_step, quarter, levels - 1, size if piece else 0, old[1] if old else 0)
                if old else functools.partial(inward_step, levels - 3),
                (*operands, stay_blocks, token),
                [VMEM] * (len(operands) + 1) + [ANY], results + [TOKEN], [VMEM] * (len(results) + 1), [], "turn", 16,
            )
            message = send(results[-1], apart(quarter))
            if piece:
                swapped[piece] = results[0], message
            if old:
                kept[old] = results[-2], message
        elif step == "relay":
            own, arrived = swapped.pop(piece)
            own, other, sent, token = call(
                functools.partial(relay_step, levels - 2),
                (own, arrived, stay_blocks, cross_blocks, theirs, token),
                [VMEM] * 5 + [ANY], [pair, pair, array(size, 4 * rank), TOKEN], [VMEM] * 4, [], "relay", 16,
            )
            kept[piece] = own, other
            across_in[piece] = send(sent, across)
        elif step == "last":
            operands = [*kept.pop(piece), out_basis, near_blocks, sources, rims["chip"], rims["middle"],
                        rims["next"], token]
            in_specs = [VMEM] * 8 + [ANY]
            aliases = {}
            if out is not None:
                operands.append(out)
                in_specs.append(ANY)
                aliases = {9: 0}
            out, token = call(
                functools.partial(last_step, quarter, start, size),
                operands, in_specs,
                [jax.ShapeDtypeStruct((rows, points), F32), TOKEN],
                [pl.BlockSpec(memory_space=pltpu.HBM), VMEM],
                [pltpu.VMEM((size, points + 2 * rim), BF16), pltpu.VMEM((size, points), F32),
                 sems(len(blocks_of(size)))],
                "last", 16, aliases,
            )
        elif step == "take":
            (token,) = call(take_step, (rims[piece], token), [ANY] * 2, [TOKEN], [VMEM], [], "take", 8)
        else:
            to, token = call(
                functools.partial(rim_step, piece == "chip"), (sources, token), [VMEM, ANY],
                [array(rows, rim), TOKEN], [VMEM] * 2, [], "rims", 8,
            )
            rims[piece] = send(to, {"chip": apart(1), "middle": middle, "next": next_over}[piece])
    return out


def solution(mesh):
    in_specs = (
        P(None, "box"),
        P("box", None, None),
        P(None, "box", None, None),
        P(None, "box", None, None),
        P("box", None, None),
        P("box", None, None),
    )
    out_specs = P(None, "box")
    return jax.shard_map(
        per_device, mesh=mesh, in_specs=in_specs, out_specs=out_specs, check_vma=False
    )
```

```python
import functools

import jax
import jax.numpy as jnp
from jax import lax
from jax.experimental import pallas as pl
from jax.experimental.pallas import tpu as pltpu
from jax.sharding import PartitionSpec as P

BF16 = jnp.bfloat16
F32 = jnp.float32
SHARES = (15, 21, 26, 29, 25, 12)


def dot(a, b):
    return jnp.dot(a, b, preferred_element_type=F32)


def cut(rows, shares):
    ends = [rows * sum(shares[: at + 1]) // sum(shares) // 16 * 16 for at in range(len(shares))]
    ends[-1] = rows
    starts = [0] + ends[:-1]
    return [(start, end - start) for start, end in zip(starts, ends)]


def order_of(pieces, inward):
    count = len(pieces)
    order = [("leaf", pieces[0]), ("level", pieces[0], 1), ("leaf", pieces[1]), ("rims", "chip")]
    arrived, landed = [], []
    for turn in range(2, count + inward + 2):
        new, old = turn - inward, turn - inward - 2
        if turn == inward:
            order.append(("take", "chip"))
        if new >= 0 and new != 1:
            order.append(("turn", pieces[new] if new < count else None, pieces[old] if old >= 0 else None))
        if turn > count:
            order += [("take", "next")] if turn == count + 1 else []
            order += [("last", piece) for piece in arrived]
            arrived = []
        for level in range(inward - 1, 0, -1):
            if turn == inward + 1 and level == 1:
                order.append(("take", "middle"))
            if 0 <= turn - level < count:
                order.append(("level", pieces[turn - level], level))
        if turn == inward:
            order += [("rims", "middle"), ("turn", pieces[1], None), ("relay", pieces[new])]
        if turn == inward + 1:
            order.append(("relay", pieces[new]))
        if turn < count:
            order.append(("leaf", pieces[turn]))
        if turn == count:
            order.append(("rims", "next"))
        if inward + 1 < turn and new < count:
            order.append(("relay", pieces[new]))
        if old >= 0:
            arrived.append(pieces[old])
    return order + [("last", piece) for piece in arrived]


def copies(pairs, sems):
    return [pltpu.make_async_copy(src, dst, sems.at[at]) for at, (src, dst) in enumerate(pairs)]


def blocks_of(size):
    step = 128
    return [(at, min(step, size - at)) for at in range(0, size, step)]


def leaf_rows(src, leaf, stay, cross, held, sent, rows):
    points, rank = leaf.shape[1:]
    grown = [
        dot(src[rows, b * points : (b + 1) * points].astype(BF16), leaf[b]).astype(BF16) for b in range(2)
    ]
    for b in range(2):
        cols = slice(b * rank, (b + 1) * rank)
        mixed = (dot(grown[b], stay[0, b]) + dot(grown[1 - b], cross[0, 1 - b])).astype(BF16)
        held[:, cols] = mixed
        sent[:, cols] = dot(mixed, cross[1, b]).astype(BF16)


def first_leaf_step(size, level, src, leaf, stay, cross, prev, held, sent, packed, token, rows, leaf_in, stay_in, cross_in, sems):
    moves = copies(
        [
            *[(src.at[pl.ds(at, n)], rows.at[pl.ds(at, n)]) for at, n in blocks_of(size)],
            (leaf.at[0], leaf_in.at[0]),
            (leaf.at[1], leaf_in.at[1]),
            (stay.at[pl.ds(0, 1)], stay_in),
            (cross.at[pl.ds(0, 2)], cross_in),
            (cross.at[pl.ds(level, 2)], packed.at[pl.ds(0, 2)]),
            (stay.at[pl.ds(level, 2)], packed.at[pl.ds(2, 2)]),
        ],
        sems,
    )
    for move in moves:
        move.start()
    for move in moves[:-2]:
        move.wait()
    leaf_rows(rows, leaf_in, stay_in, cross_in, held, sent, slice(None))
    for move in moves[-2:]:
        move.wait()
    token[...] = jnp.zeros_like(token)


def leaf_step(start, size, src, leaf, stay, cross, prev, *outs):
    held, sent, token = outs[-3:]
    leaf_rows(src, leaf, stay, cross, held, sent, slice(start, start + size))
    token[...] = jnp.zeros_like(token)


def mix(held, moved, block):
    return (dot(held, block) + moved.astype(F32)).astype(BF16)


def level_step(level, held_in, moved, stay, cross, prev, held, sent, token):
    rank = stay.shape[-1]
    for b in range(2):
        cols = slice(b * rank, (b + 1) * rank)
        mixed = mix(held_in[:, cols], moved[:, cols], stay[level, b])
        held[:, cols] = mixed
        sent[:, cols] = dot(mixed, cross[level + 1, b]).astype(BF16)
    token[...] = jnp.zeros_like(token)


def relay_step(level, own, other, stay, cross, theirs_in, prev, own_out, other_out, sent, token):
    rank = stay.shape[-1]
    width = 2 * rank
    size = own.shape[0]
    for b in range(2):
        cols = slice(b * rank, (b + 1) * rank)
        mine, theirs = own[:, cols], other[:size, cols]
        theirs_mixed = (dot(theirs, theirs_in[2, b]) + dot(mine, cross[level, b])).astype(BF16)
        sent[:, cols] = dot(theirs_mixed, theirs_in[1, b]).astype(BF16)
        other_out[:, cols] = theirs_mixed
        mine_mixed = (dot(mine, stay[level, b]) + dot(theirs, theirs_in[0, b])).astype(BF16)
        sent[:, width + b * rank : width + (b + 1) * rank] = dot(mine_mixed, cross[level + 1, b]).astype(BF16)
        own_out[:, cols] = mine_mixed
    token[...] = jnp.zeros_like(token)


def inward_step(level, held_in, moved, stay, prev, held, token):
    rank = stay.shape[-1]
    for b in range(2):
        cols = slice(b * rank, (b + 1) * rank)
        held[:, cols] = mix(held_in[:, cols], moved[:, cols], stay[level, b])
    token[...] = jnp.zeros_like(token)


def turn_step(quarter, level, new, old, *refs):
    refs = list(refs)
    if new:
        held_in, moved = refs.pop(0), refs.pop(0)
    if old:
        own, other, across, theirs_in = (refs.pop(0) for _ in range(4))
    stay, prev = refs.pop(0), refs.pop(0)
    token = refs.pop()
    rank = stay.shape[-1]
    width = 2 * rank
    me = lax.axis_index("box")
    inner = jnp.logical_and(me >= quarter, me < 3 * quarter)
    sent = refs.pop()
    for b in range(2):
        cols = slice(b * rank, (b + 1) * rank)
        shifted = slice(width + b * rank, width + (b + 1) * rank)
        if new:
            going_in = mix(held_in[:, cols], moved[:, cols], stay[level - 2, b])
            refs[0][:, cols] = going_in
        if old:
            refs[-1][:, cols] = mix(own[:, cols], across[:, cols], stay[level, b])
            going_out = mix(other[:, cols], across[:, shifted], theirs_in[3, b])
        if new and old:
            both = min(new, old)
            sent[:both, cols] = jnp.where(inner, going_out[:both], going_in[:both])
            if new > both:
                sent[both:, cols] = going_in[both:]
            if old > both:
                sent[both:, cols] = going_out[both:]
        elif old:
            sent[:, cols] = going_out
    token[...] = jnp.zeros_like(token)


def last_step(quarter, start, size, own, back, out_basis, near, src, rim_a, rim_m, rim_n, prev, *refs):
    out, token, window, result, sems = refs[-5:]
    rank, points = out_basis.shape[1:]
    rim = rim_a.shape[1]
    blocks = blocks_of(size)
    me = lax.axis_index("box")
    odd = lax.rem(me, 2) == 1
    inner = jnp.logical_and(me >= quarter, me < 3 * quarter)
    halfway = jnp.logical_or(me == 2 * quarter - 1, me == 2 * quarter)
    leaves = copies([(result.at[pl.ds(at, n)], out.at[pl.ds(start + at, n)]) for at, n in blocks], sems)
    for leave, (at, n) in zip(leaves, blocks):
        part, whole = slice(at, at + n), slice(start + at, start + at + n)
        rim_b = jnp.where(halfway, rim_m[whole], rim_n[whole])
        before, after = jnp.where(odd, rim_a[whole], rim_b), jnp.where(odd, rim_b, rim_a[whole])
        window[part, :rim] = before
        window[part, rim : rim + 2 * points] = src[whole].astype(BF16)
        window[part, rim + 2 * points :] = after
        for b in range(2):
            cols = slice(b * rank, (b + 1) * rank)
            mixed = jnp.where(inner, own[part, cols], back[part, cols])
            result[part, b * points : (b + 1) * points] = dot(mixed, out_basis[b]) + dot(
                window[part, b * points : (b + 1) * points + 2 * rim], near[b]
            )
        leave.start()
    for leave in leaves:
        leave.wait()
    token[...] = jnp.zeros_like(token)


def rim_step(swap, src, prev, to, token):
    rim = to.shape[1]
    odd = lax.rem(lax.axis_index("box"), 2) == int(swap)
    head, tail = src[:, :rim].astype(BF16), src[:, src.shape[1] - rim :].astype(BF16)
    to[...] = jnp.where(odd, head, tail)
    token[...] = jnp.zeros_like(token)


def take_step(*refs):
    token = refs[-1]
    token[...] = jnp.zeros_like(token)


ANY = pl.BlockSpec(memory_space=pl.ANY)
VMEM = pl.BlockSpec(memory_space=pltpu.VMEM)
TOKEN = jax.ShapeDtypeStruct((8, 128), F32)
SOME = pl.CostEstimate(flops=3 * 10**9, bytes_accessed=1, transcendentals=0)
LITTLE = pl.CostEstimate(flops=10**7, bytes_accessed=1, transcendentals=0)


LIGHT = ("last", "relay")


def call(body, operands, in_specs, out_shape, out_specs, scratch, name, mib, aliases=None):
    return pl.pallas_call(
        body,
        in_specs=in_specs,
        out_specs=out_specs,
        out_shape=out_shape,
        scratch_shapes=scratch,
        input_output_aliases=aliases or {},
        compiler_params=pltpu.CompilerParams(vmem_limit_bytes=mib * 1024 * 1024),
        cost_estimate=LITTLE if name in LIGHT else SOME,
        name=name,
    )(*operands)


def per_device(sources, leaf_basis, stay_blocks, cross_blocks, out_basis, near_blocks):
    rows, points = sources.shape
    levels, _, rank, _ = stay_blocks.shape
    devices = lax.axis_size("box")
    quarter = devices // 4
    inward = levels - 3
    rim = (near_blocks.shape[1] - near_blocks.shape[2]) // 2
    pieces = cut(rows, SHARES)
    array = lambda *shape: jax.ShapeDtypeStruct(shape, BF16)
    sems = lambda count: pltpu.SemaphoreType.DMA((count,))
    in_hbm = lambda operand: pltpu.with_memory_space_constraint(operand, pltpu.HBM)
    apart = lambda gap: [(i, i ^ gap) for i in range(devices)]
    across = [
        (i, i ^ 3 * quarter if quarter <= i < 3 * quarter else i ^ 1) for i in range(devices)
    ]
    middle = [(devices // 2 - 1, devices // 2), (devices // 2, devices // 2 - 1)]
    next_over = [(i, (i - 1 ^ 1) + 1) for i in range(1, devices - 1)]
    next_over = [link for link in next_over if link not in middle]
    send = lambda operand, pairs: lax.ppermute(operand, "box", pairs)
    small = tuple(stay_blocks.shape[1:])

    token = jnp.zeros(TOKEN.shape, TOKEN.dtype)
    out, theirs = None, None
    held, moved, kept, across_in, swapped, rims = {}, {}, {}, {}, {}, {}
    for step, *rest in order_of(pieces, inward):
        piece = rest[0] if rest else None
        start, size = piece if isinstance(piece, tuple) else (0, rows)
        pair = array(size, 2 * rank)
        if step == "leaf" and start == 0:
            held[1, piece], sent, packed, token = call(
                functools.partial(first_leaf_step, size, levels - 2),
                (*map(in_hbm, (sources, leaf_basis, stay_blocks, cross_blocks)), token),
                [ANY] * 5, [pair, pair, array(4, *small), TOKEN], [VMEM] * 4,
                [pltpu.VMEM((size, points), F32), pltpu.VMEM(leaf_basis.shape, BF16),
                 pltpu.VMEM((1,) + small, BF16), pltpu.VMEM((2,) + small, BF16), sems(6 + len(blocks_of(size)))],
                "leaf", 16,
            )
            moved[1, piece] = send(sent, apart(1))
            theirs = send(packed, apart(quarter))
        elif step == "leaf":
            held[1, piece], sent, token = call(
                functools.partial(leaf_step, start, size),
                (sources, leaf_basis, stay_blocks, cross_blocks, token),
                [VMEM] * 4 + [ANY], [pair, pair, TOKEN], [VMEM] * 3, [], "leaf", 16,
            )
            moved[1, piece] = send(sent, apart(1))
        elif step == "level":
            level = rest[1]
            held[level + 1, piece], sent, token = call(
                functools.partial(level_step, level),
                (held.pop((level, piece)), moved.pop((level, piece)), stay_blocks, cross_blocks, token),
                [VMEM] * 4 + [ANY], [pair, pair, TOKEN], [VMEM] * 3, [], "level", 16,
            )
            moved[level + 1, piece] = send(sent, apart(1 << level))
        elif step == "turn":
            old = rest[1]
            operands, results = (), []
            if piece:
                operands += held.pop((inward, piece)), moved.pop((inward, piece))
                results.append(pair)
            if old:
                operands += (*kept.pop(old), across_in.pop(old), theirs)
                results.append(array(old[1], 2 * rank))
            if old or not piece:
                results.append(array(max(size if piece else 0, old[1]), 2 * rank))
            *results, token = call(
                functools.partial(turn_step, quarter, levels - 1, size if piece else 0, old[1] if old else 0)
                if old else functools.partial(inward_step, levels - 3),
                (*operands, stay_blocks, token),
                [VMEM] * (len(operands) + 1) + [ANY], results + [TOKEN], [VMEM] * (len(results) + 1), [], "turn", 16,
            )
            message = send(results[-1], apart(quarter))
            if piece:
                swapped[piece] = results[0], message
            if old:
                kept[old] = results[-2], message
        elif step == "relay":
            own, arrived = swapped.pop(piece)
            own, other, sent, token = call(
                functools.partial(relay_step, levels - 2),
                (own, arrived, stay_blocks, cross_blocks, theirs, token),
                [VMEM] * 5 + [ANY], [pair, pair, array(size, 4 * rank), TOKEN], [VMEM] * 4, [], "relay", 16,
            )
            kept[piece] = own, other
            across_in[piece] = send(sent, across)
        elif step == "last":
            operands = [*kept.pop(piece), out_basis, near_blocks, sources, rims["chip"], rims["middle"],
                        rims["next"], token]
            in_specs = [VMEM] * 8 + [ANY]
            aliases = {}
            if out is not None:
                operands.append(out)
                in_specs.append(ANY)
                aliases = {9: 0}
            out, token = call(
                functools.partial(last_step, quarter, start, size),
                operands, in_specs,
                [jax.ShapeDtypeStruct((rows, points), F32), TOKEN],
                [pl.BlockSpec(memory_space=pltpu.HBM), VMEM],
                [pltpu.VMEM((size, points + 2 * rim), BF16), pltpu.VMEM((size, points), F32),
                 sems(len(blocks_of(size)))],
                "last", 16, aliases,
            )
        elif step == "take":
            (token,) = call(take_step, (rims[piece], token), [ANY] * 2, [TOKEN], [VMEM], [], "take", 8)
        else:
            to, token = call(
                functools.partial(rim_step, piece == "chip"), (sources, token), [VMEM, ANY],
                [array(rows, rim), TOKEN], [VMEM] * 2, [], "rims", 8,
            )
            rims[piece] = send(to, {"chip": apart(1), "middle": middle, "next": next_over}[piece])
    return out


def solution(mesh):
    in_specs = (
        P(None, "box"),
        P("box", None, None),
        P(None, "box", None, None),
        P(None, "box", None, None),
        P("box", None, None),
        P("box", None, None),
    )
    out_specs = P(None, "box")
    return jax.shard_map(
        per_device, mesh=mesh, in_specs=in_specs, out_specs=out_specs, check_vma=False
    )
```
